32 devices in a mesh: tile: 8 (over z, x), dp: 4 (over y, core).
Axes of the slice: x: 2, y: 2, z: 4, core: 2. Of those that a mesh axis runs over, the one named last changes fastest.
Arguments:
- fields: bfloat16 [4, 16, 64, 64, 128], P('dp', 'tile'), may hold values from -6 to 6
- cotangent: bfloat16 [4, 16, 64, 64, 128], P('dp', 'tile'), may hold values from -6 to 6
- is_ocean: int32 [16], P('tile'), may hold values from 0 to 1, as said below
- neighbours: int32 [16, 8], P('tile'), may hold values from -1 to 15, as said below
- kernel: float32 [7, 7, 128], replicated, may hold values from -0.875 to 0.875
- conv_bias: float32 [128], replicated, may hold values from -3 to 3
- ln_gain: float32 [128], replicated, may hold values from 0.25 to 1.75
- ln_bias: float32 [128], replicated, may hold values from -3 to 3
- w_up: bfloat16 [128, 512], replicated, may hold values from -0.5 to 0.5
- up_bias: float32 [512], replicated, may hold values from -3 to 3
- w_down: bfloat16 [512, 128], replicated, may hold values from -0.25 to 0.25
- down_bias: float32 [128], replicated, may hold values from -3 to 3
- layer_scale: float32 [128], replicated, may hold values from 0.3 to 1
Outputs:
- grad_fields: bfloat16 [4, 16, 64, 64, 128], P('dp', 'tile')
- g_kernel: float32 [7, 7, 128], replicated
- g_conv_bias: float32 [128], replicated
- g_ln_gain: float32 [128], replicated
- g_ln_bias: float32 [128], replicated
- g_w_up: float32 [128, 512], replicated
- g_up_bias: float32 [512], replicated
- g_w_down: float32 [512, 128], replicated
- g_down_bias: float32 [128], replicated
- g_layer_scale: float32 [128], replicated
The draws below stay inside these ranges and needn't reach their ends.
Inputs may be any that keep to these rules, and one draw needn't show every extreme that they name: `is_ocean`: slots follow a serpentine curve through the columns of a grid of 8 x 2 tiles, alternating direction from column to column; tiles of the first and last grid rows are ocean. Entry k of slot s names the slot of the tile adjacent in direction k (north, south, west, east, north-west, north-east, south-west, south-east), or -1 where that tile is land or outside the grid or slot s is land; the relation is symmetric; the north and south neighbours are slot s - 1 or s + 1, and every neighbour lies within 15 slots of s.
All inputs are finite; a program needn't handle non-finite values.
Results may differ from the reference program's by a relative error of at most 0.0071.
Values may be sent and summed in bfloat16 or wider, within the bound.
A program may use at most 128 MiB of HBM per device.

```python
import math
import jax
import jax.numpy as jnp
from jax import lax

CH = 128
HIDDEN_SIZE = 512
TILE = 64
TROWS = 8
SLOTS = 16
TCOLS = 2
SAMPLES = 4


def plan_draw(key):
    base_key = jax.random.fold_in(key, 7321)
    land_key, flip_key, row_key, column_key = jax.random.split(base_key, 4)
    land_mask = jax.random.randint(land_key, (TROWS, TCOLS), 0, 4) == 0
    row_ids = jnp.arange(TROWS)[:, None]
    column_ids = jnp.arange(TCOLS)[None, :]
    forced_row = jax.random.randint(row_key, (), 1, TROWS - 1)
    forced_column = jax.random.randint(column_key, (), 0, TCOLS)
    land_mask = land_mask | (row_ids == forced_row) & (column_ids == forced_column)
    land_mask = land_mask & (row_ids > 0) & (row_ids < TROWS - 1)
    flip_bit = jax.random.randint(flip_key, (), 0, 2)
    downward = (jnp.arange(TCOLS) + flip_bit) % 2 == 0
    slot_ids = jnp.arange(SLOTS)
    column = slot_ids // TROWS
    along = slot_ids % TROWS
    grid_row = jnp.where(downward[column], along, TROWS - 1 - along)
    ocean = jnp.logical_not(land_mask[grid_row, column])
    offsets = [(-1, 0), (1, 0), (0, -1), (0, 1), (-1, -1), (-1, 1), (1, -1), (1, 1)]
    columns_out = []
    for row_step, col_step in offsets:
        target_row = grid_row + row_step
        target_column = column + col_step
        inside = (target_row >= 0) & (target_row < TROWS) & (target_column >= 0) & (target_column < TCOLS)
        clipped_row = jnp.clip(target_row, 0, TROWS - 1)
        clipped_column = jnp.clip(target_column, 0, TCOLS - 1)
        linked = inside & jnp.logical_not(land_mask[clipped_row, clipped_column]) & ocean
        target_slot = clipped_column * TROWS + jnp.where(downward[clipped_column], clipped_row, TROWS - 1 - clipped_row)
        columns_out.append(jnp.where(linked, target_slot, -1))
    return (ocean.astype(jnp.int32), jnp.stack(columns_out, 1).astype(jnp.int32))


def draw_is_ocean(key, part):
    return plan_draw(key)[0]


def draw_neighbours(key, part):
    return plan_draw(key)[1]


def block_scale(stream_key, shape, shards, smallest, high):
    def one(axis_at, shards_of):
        steps = jax.random.uniform(jax.random.fold_in(jax.random.fold_in(stream_key, 6), axis_at), (shards_of,), jnp.float32, smallest / len(shards), high / len(shards))
        return jnp.repeat(jnp.exp(steps), shape[axis_at] // shards_of).reshape((-1,) + (1,) * (len(shape) - axis_at - 1))

    factor_of = one(*shards[0])
    for cut in shards[1:]:
        factor_of = factor_of * one(*cut)
    return factor_of


def bell_draw(own_key, shape, scale, most, pieces=(), held_as=jnp.bfloat16):
    values = scale * jax.random.normal(own_key, shape, jnp.float32)
    if pieces:
        values = values * block_scale(own_key, shape, pieces, -0.22, 0.18)
    return jnp.clip(values, -most, most).astype(held_as)


def setup_inputs(seed: int = 0) -> dict:
    key_of = jax.random.split(jax.random.key(seed), 14)
    fields = bell_draw(key_of[0], (SAMPLES, SLOTS, TILE, TILE, CH), 1.0, 6.0, ((0, 4), (1, 8)))
    cotangent = bell_draw(key_of[1], (SAMPLES, SLOTS, TILE, TILE, CH), 1.0, 6.0, ((0, 4), (1, 8)))
    is_ocean = draw_is_ocean(jax.random.fold_in(key_of[13], 71), 0)
    neighbours = draw_neighbours(jax.random.fold_in(key_of[13], 71), 0)
    kernel = bell_draw(key_of[4], (7, 7, CH), 49 ** -0.5, 0.875, (), jnp.float32)
    conv_bias = bell_draw(key_of[5], (CH,), 0.5, 3.0, (), jnp.float32)
    ln_gain = jnp.clip(1.0 + 0.15 * jax.random.normal(key_of[6], (CH,), jnp.float32), 0.25, 1.75)
    ln_bias = bell_draw(key_of[7], (CH,), 0.5, 3.0, (), jnp.float32)
    w_up = bell_draw(key_of[8], (CH, HIDDEN_SIZE), CH ** -0.5, 0.5)
    up_bias = bell_draw(key_of[9], (HIDDEN_SIZE,), 0.5, 3.0, (), jnp.float32)
    w_down = bell_draw(key_of[10], (HIDDEN_SIZE, CH), HIDDEN_SIZE ** -0.5, 0.25)
    down_bias = bell_draw(key_of[11], (CH,), 0.5, 3.0, (), jnp.float32)
    layer_scale = jnp.clip(jnp.exp(jax.random.uniform(key_of[12], (CH,), jnp.float32, math.log(0.3), math.log(1.0))), 0.3, 1.0)
    return {"fields": fields, "cotangent": cotangent, "is_ocean": is_ocean, "neighbours": neighbours, "kernel": kernel, "conv_bias": conv_bias, "ln_gain": ln_gain, "ln_bias": ln_bias, "w_up": w_up, "up_bias": up_bias, "w_down": w_down, "down_bias": down_bias, "layer_scale": layer_scale}


EPSILON = 1e-06

def rims_of(tile_block, rim_depth):
    extent = tile_block.shape[0]
    top_band = tile_block[:rim_depth]
    bottom = tile_block[extent - rim_depth:]
    left_band = jnp.transpose(tile_block[:, :rim_depth], (1, 0, 2))
    right_band = jnp.transpose(tile_block[:, extent - rim_depth:], (1, 0, 2))
    return jnp.stack([top_band, bottom, left_band, right_band], 0)

def assemble(own_tile, picked, valid_flags, first_layer, rim_depth):
    extent = own_tile.shape[0]

    def rim_piece(direction, which_strip):
        stripe = picked[direction][which_strip, first_layer:first_layer + rim_depth]
        return stripe * valid_flags[direction].astype(own_tile.dtype)
    north_rim = rim_piece(0, 1)
    south_rim = rim_piece(1, 0)
    west_rim = jnp.transpose(rim_piece(2, 1), (1, 0, 2))
    east_rim = jnp.transpose(rim_piece(3, 0), (1, 0, 2))
    north_west = jnp.transpose(rim_piece(4, 1)[:, extent - rim_depth:], (1, 0, 2))
    north_east = jnp.transpose(rim_piece(5, 0)[:, extent - rim_depth:], (1, 0, 2))
    south_west = jnp.transpose(rim_piece(6, 1)[:, :rim_depth], (1, 0, 2))
    south_east = jnp.transpose(rim_piece(7, 0)[:, :rim_depth], (1, 0, 2))
    top_band = jnp.concatenate([north_west, north_rim, north_east], 1)
    middle = jnp.concatenate([west_rim, own_tile, east_rim], 1)
    bottom = jnp.concatenate([south_west, south_rim, south_east], 1)
    return jnp.concatenate([top_band, middle, bottom], 0)

def depthwise(padded, kernel, extent):
    running_sum = jnp.zeros((extent, extent, padded.shape[2]), jnp.float32)
    for lag_row in range(7):
        for lag_col in range(7):
            window = padded[lag_row:lag_row + extent, lag_col:lag_col + extent].astype(jnp.float32)
            running_sum = running_sum + window * kernel[lag_row, lag_col]
    return running_sum

def transposed(grad_padded, kernel, extent):
    running_sum = jnp.zeros((extent, extent, grad_padded.shape[2]), jnp.float32)
    for lag_row in range(7):
        for lag_col in range(7):
            window = grad_padded[6 - lag_row:6 - lag_row + extent, 6 - lag_col:6 - lag_col + extent].astype(jnp.float32)
            running_sum = running_sum + window * kernel[lag_row, lag_col]
    return running_sum

def kernel_terms(grad_tile, padded, extent):
    grad_values = grad_tile.astype(jnp.float32)
    stacked = []
    for lag_row in range(7):
        line_terms = []
        for lag_col in range(7):
            window = padded[lag_row:lag_row + extent, lag_col:lag_col + extent].astype(jnp.float32)
            line_terms.append(lax.optimization_barrier(jnp.sum(grad_values * window, axis=(0, 1))))
        stacked.append(jnp.stack(line_terms, 0))
    return jnp.stack(stacked, 0)

def gelu_tanh(values):
    return jax.nn.gelu(values, approximate=True)

def layer_rows(conv_rows, cot_rows, ln_gain, ln_bias, w_up, up_bias, w_down, down_bias, layer_scale):
    mean_value = lax.optimization_barrier(jnp.mean(conv_rows, -1, keepdims=True))
    centred = conv_rows - mean_value
    variance = lax.optimization_barrier(jnp.mean(centred * centred, -1, keepdims=True))
    inverse_scale = lax.rsqrt(variance + EPSILON)
    normed = centred * inverse_scale
    scaled = (normed * ln_gain + ln_bias).astype(jnp.bfloat16)
    hidden_sum = jnp.dot(scaled, w_up, preferred_element_type=jnp.float32) + up_bias
    activation = gelu_tanh(hidden_sum).astype(jnp.bfloat16)
    mixed = jnp.dot(activation, w_down, preferred_element_type=jnp.float32) + down_bias
    grad_mixed = (cot_rows * layer_scale).astype(jnp.bfloat16)
    grad_act = jnp.dot(grad_mixed, w_down.T, preferred_element_type=jnp.float32)
    pullback = jax.vjp(gelu_tanh, hidden_sum)[1]
    grad_pre = pullback(grad_act)[0].astype(jnp.bfloat16)
    grad_scaled = jnp.dot(grad_pre, w_up.T, preferred_element_type=jnp.float32)
    grad_normed = grad_scaled * ln_gain
    grad_conv = inverse_scale * (grad_normed - lax.optimization_barrier(jnp.mean(grad_normed, -1, keepdims=True)) - normed * lax.optimization_barrier(jnp.mean(grad_normed * normed, -1, keepdims=True)))
    return (grad_conv.astype(jnp.bfloat16), mixed, grad_mixed, activation, grad_pre, scaled, grad_scaled, normed)

def row_terms(cot_rows, mixed, grad_mixed, activation, grad_pre, scaled, grad_scaled, normed, grad_conv):
    return (lax.optimization_barrier(jnp.sum(grad_conv.astype(jnp.float32), 0)), lax.optimization_barrier(jnp.sum(grad_scaled * normed, 0)), lax.optimization_barrier(jnp.sum(grad_scaled, 0)), jnp.dot(scaled.T, grad_pre, preferred_element_type=jnp.float32), lax.optimization_barrier(jnp.sum(grad_pre.astype(jnp.float32), 0)), jnp.dot(activation.T, grad_mixed, preferred_element_type=jnp.float32), lax.optimization_barrier(jnp.sum(grad_mixed.astype(jnp.float32), 0)), lax.optimization_barrier(jnp.sum(cot_rows * mixed, 0)))

def reference(fields, cotangent, is_ocean, neighbours, kernel, conv_bias, ln_gain, ln_bias, w_up, up_bias, w_down, down_bias, layer_scale):
    samples, slot_count, extent, channels = (fields.shape[0], fields.shape[1], fields.shape[2], fields.shape[4])
    hidden_width = w_up.shape[1]
    grad_sums = (jnp.zeros((7, 7, channels), jnp.float32), jnp.zeros((channels,), jnp.float32), jnp.zeros((channels,), jnp.float32), jnp.zeros((channels,), jnp.float32), jnp.zeros((channels, hidden_width), jnp.float32), jnp.zeros((hidden_width,), jnp.float32), jnp.zeros((hidden_width, channels), jnp.float32), jnp.zeros((channels,), jnp.float32), jnp.zeros((channels,), jnp.float32))
    outputs = []
    for sample in range(samples):
        tile_stack = fields[sample]
        cot_stack = cotangent[sample]
        rims_x = jax.vmap(lambda tile_block: rims_of(tile_block, 3))(tile_stack)

        def fetch_rims(rim_set, slot_ids):
            safe_ids = jnp.maximum(slot_ids, 0)
            picked = [rim_set[safe_ids[0]], rim_set[safe_ids[1]]]
            picked = picked + [rim_set[safe_ids[direction]][2:4] for direction in range(2, 8)]
            return (picked, slot_ids >= 0)

        def first_pass(running, slot_id):
            picked, valid_flags = fetch_rims(rims_x, neighbours[slot_id])
            padded = assemble(tile_stack[slot_id], picked, valid_flags, 0, 3)
            conv_out = depthwise(padded, kernel, extent) + conv_bias
            cot_rows = cot_stack[slot_id].astype(jnp.float32).reshape(-1, channels)
            layer_parts = layer_rows(conv_out.reshape(-1, channels), cot_rows, ln_gain, ln_bias, w_up, up_bias, w_down, down_bias, layer_scale)
            grad_tile = layer_parts[0].reshape(extent, extent, channels)
            weight_terms = (kernel_terms(grad_tile, padded, extent),) + row_terms(cot_rows, *layer_parts[1:], layer_parts[0])
            keep_flag = (is_ocean[slot_id] > 0).astype(jnp.float32)
            running = tuple((total + keep_flag * term for total, term in zip(running, weight_terms)))
            return (running, grad_tile)
        grad_sums, grad_all = lax.scan(first_pass, grad_sums, jnp.arange(slot_count))
        rims_g = jax.vmap(lambda tile_block: rims_of(tile_block, 3))(grad_all)

        def second_pass(slot_id):
            picked, valid_flags = fetch_rims(rims_g, neighbours[slot_id])
            grad_padded = assemble(grad_all[slot_id], picked, valid_flags, 0, 3)
            result = cot_stack[slot_id].astype(jnp.float32) + transposed(grad_padded, kernel, extent)
            keep_flag = (is_ocean[slot_id] > 0).astype(jnp.float32)
            return (result * keep_flag).astype(jnp.bfloat16)
        outputs.append(lax.map(second_pass, jnp.arange(slot_count)))
    grad_scale = 1.0 / float(samples * slot_count * extent * extent) ** 0.5
    return (jnp.stack(outputs, 0), grad_sums[0] * grad_scale, grad_sums[1] * grad_scale, grad_sums[2] * grad_scale, grad_sums[3] * grad_scale, grad_sums[4] * grad_scale, grad_sums[5] * grad_scale, grad_sums[6] * grad_scale, grad_sums[7] * grad_scale, grad_sums[8] * grad_scale)
```

```python
from functools import partial
import math

import jax
import jax.numpy as jnp
from jax import lax
from jax.experimental import pallas as pl
from jax.experimental.pallas import tpu as pltpu
from jax.sharding import PartitionSpec as P

TROWS = 8
EPSILON = 1e-06
BF = jnp.bfloat16
F32 = jnp.float32
MESH = pl.DeviceIdType.MESH
PAIRS = 4
WEST = 5
VMEM_BYTES = 56 * 1024 * 1024


def halo_kernel(per_column, sv, ss, sc, rv, rs, rc, send_sems, recv_sems):
    tile_count = lax.axis_size("tile")
    me = lax.axis_index("tile")
    dp = lax.axis_index("dp")
    columns = tile_count // per_column
    col = me // per_column
    row = me % per_column
    mirror = per_column - 1 - row
    west = (col - 1) * per_column + mirror
    east = (col + 1) * per_column + mirror
    has_prev = row > 0
    has_next = row < per_column - 1
    has_west = col > 0
    has_east = col < columns - 1
    jobs = [
        (has_west, west, ss.at[0], rs.at[1], has_east),
        (has_east, east, ss.at[1], rs.at[0], has_west),
        (has_next, me + 1, sv.at[0], rv.at[0], has_prev),
        (has_prev, me - 1, sv.at[1], rv.at[1], has_next),
        (has_west & has_prev, west + 1, sc.at[0, 0], rc.at[1, 0], has_east & has_prev),
        (has_west & has_next, west - 1, sc.at[0, 1], rc.at[1, 1], has_east & has_next),
        (has_east & has_prev, east + 1, sc.at[1, 0], rc.at[0, 0], has_west & has_prev),
        (has_east & has_next, east - 1, sc.at[1, 1], rc.at[0, 1], has_west & has_next),
    ]
    barrier = pltpu.get_barrier_semaphore()
    for sends, target, _, _, _ in jobs:

        @pl.when(sends)
        def _(target=target):
            pl.semaphore_signal(barrier, inc=1, device_id=(target, dp), device_id_type=MESH)

    peers = sum(sends.astype(jnp.int32) for sends, _, _, _, _ in jobs)
    pl.semaphore_wait(barrier, peers)

    def copy_of(index):
        _, target, source, destination, _ = jobs[index]
        return pltpu.make_async_remote_copy(
            src_ref=source,
            dst_ref=destination,
            send_sem=send_sems.at[index],
            recv_sem=recv_sems.at[index],
            device_id=(target, dp),
            device_id_type=MESH,
        )

    for index in range(len(jobs)):

        @pl.when(jobs[index][0])
        def _(index=index):
            copy_of(index).start()

    for index in range(len(jobs)):

        @pl.when(jobs[index][4])
        def _(index=index):
            copy_of(index).wait_recv()

        @pl.when(jobs[index][0])
        def _(index=index):
            copy_of(index).wait_send()


def exchange(packed, per_column, collective_id):
    any_spec = pl.BlockSpec(memory_space=pl.ANY)
    return pl.pallas_call(
        partial(halo_kernel, per_column),
        out_shape=tuple(jax.ShapeDtypeStruct(part.shape, part.dtype) for part in packed),
        in_specs=[any_spec] * 3,
        out_specs=(any_spec,) * 3,
        scratch_shapes=[pltpu.SemaphoreType.DMA((8,)), pltpu.SemaphoreType.DMA((8,))],
        compiler_params=pltpu.CompilerParams(collective_id=collective_id, has_side_effects=True),
    )(*packed)


def pack(tiles, down):
    extent = tiles.shape[1]
    first, last = tiles[0], tiles[1]
    to_next = jnp.where(down, last[extent - 3 :], last[:3])
    to_prev = jnp.where(down, first[:3], first[extent - 3 :])
    vertical = jnp.stack([to_next, to_prev], 0)
    west = jnp.transpose(tiles[:, :, :3], (0, 2, 1, 3))
    east = jnp.transpose(tiles[:, :, extent - 3 :], (0, 2, 1, 3))
    sides = jnp.stack([west, east], 0)
    low, high = sides[:, :, :, :16], sides[:, :, :, extent - 16 :]
    corner_prev = jnp.where(down, low[:, 0], high[:, 0])
    corner_next = jnp.where(down, high[:, 1], low[:, 1])
    return vertical, sides, jnp.stack([corner_prev, corner_next], 1)


def build_windows(flags, slot, tiles, rv, rs, rc, padded, windows):
    extent = tiles.shape[1]
    width = padded.shape[1]
    down = flags[2, 0] > 0
    first = slot == 0

    def valid(direction, value):
        return jnp.where(flags[slot, direction] > 0, value, jnp.zeros_like(value))

    own = tiles.at[slot]
    other = tiles.at[1 - slot]
    padded[3 : 3 + extent, 8 : 8 + extent, :] = own[...].astype(F32)
    outer = rv[slot].astype(F32)
    inner_is_south = first == down
    inner = jnp.where(inner_is_south, other[:3], other[extent - 3 :]).astype(F32)
    north = jnp.where(inner_is_south, outer, inner)
    south = jnp.where(inner_is_south, inner, outer)
    padded[0:3, 8 : 8 + extent, :] = valid(0, north)
    padded[3 + extent : 6 + extent, 8 : 8 + extent, :] = valid(1, south)
    flat = padded.reshape(padded.shape[0] * width, padded.shape[2])
    for side, base, straight, upper, lower in ((0, WEST, 2, 4, 6), (1, 8 + extent, 3, 5, 7)):
        strips = valid(straight, rs[side, 1 - slot].astype(F32))
        inner_strips = rs[side, slot].astype(F32)
        corner = rc[side, slot].astype(F32)
        above = valid(upper, jnp.where(inner_is_south, corner[:, 13:16], inner_strips[:, extent - 3 :]))
        below = valid(lower, jnp.where(inner_is_south, inner_strips[:, :3], corner[:, 0:3]))
        for column in range(3):
            flat[pl.ds(3 * width + base + column, extent, stride=width), :] = strips[column]
            for line in range(3):
                padded[line, base + column : base + column + 1, :] = above[column, line : line + 1]
                padded[3 + extent + line, base + column : base + column + 1, :] = below[
                    column, line : line + 1
                ]

    def fill(pair, carry):
        for shift in range(7):
            upper_row = padded[2 * pair, WEST + shift : WEST + shift + extent, :]
            lower_row = padded[2 * pair + 1, WEST + shift : WEST + shift + extent, :]
            windows[shift, pair] = jnp.concatenate([upper_row, lower_row], 1).astype(BF)
        return carry

    lax.fori_loop(0, (extent + 6) // 2, fill, 0)


def conv_block(windows, taps, first_pair, pairs):
    extent, lanes = windows.shape[2], windows.shape[3]
    total = None
    for shift in range(7):
        for step in range(4):
            rows = windows[shift, pl.ds(first_pair + step, pairs)].reshape(pairs * extent, lanes)
            term = jnp.dot(rows, taps[shift * 4 + step], preferred_element_type=F32)
            total = term if total is None else total + term
    return total


def split_rows(block):
    pairs = block.shape[0] // 2
    parts = [block[2 * q] for q in range(pairs)] + [block[2 * q + 1] for q in range(pairs)]
    return jnp.concatenate(parts, 0)


def first_kernel(
    flags,
    tiles,
    cot,
    rv,
    rs,
    rc,
    taps,
    vectors,
    w_up,
    up_bias,
    w_down,
    grad_out,
    g_taps,
    g_up,
    g_down,
    g_vec,
    g_hidden,
    padded,
    windows,
    grad_turned,
):
    slot = pl.program_id(0)
    extent, channels = tiles.shape[1], tiles.shape[3]
    lanes = 2 * channels
    rows = PAIRS * extent

    @pl.when(slot == 0)
    def _():
        g_taps[...] = jnp.zeros_like(g_taps)
        g_up[...] = jnp.zeros_like(g_up)
        g_down[...] = jnp.zeros_like(g_down)
        g_vec[...] = jnp.zeros_like(g_vec)
        g_hidden[...] = jnp.zeros_like(g_hidden)

    build_windows(flags, slot, tiles, rv, rs, rc, padded, windows)
    keep = flags[slot, 8] > 0
    conv_bias, ln_gain, ln_bias, layer_scale = (vectors[k : k + 1] for k in range(4))
    root = math.sqrt(2.0 / math.pi)

    def block_step(block, carry):
        total = conv_block(windows, taps, block * PAIRS, PAIRS)
        conv = jnp.concatenate([total[:, :channels], total[:, channels:]], 0) + conv_bias
        cot_rows = split_rows(cot[0, pl.ds(block * 2 * PAIRS, 2 * PAIRS)]).astype(F32)
        cot_rows = jnp.where(keep, cot_rows, jnp.zeros_like(cot_rows))
        centred = conv - jnp.mean(conv, -1, keepdims=True)
        inverse = lax.rsqrt(jnp.mean(centred * centred, -1, keepdims=True) + EPSILON)
        normed = centred * inverse
        scaled = (normed * ln_gain + ln_bias).astype(BF)
        hidden = jnp.dot(scaled, w_up[...], preferred_element_type=F32) + up_bias[...]
        grad_mixed_f = cot_rows * layer_scale
        grad_mixed = grad_mixed_f.astype(BF)
        grad_act = lax.dot_general(
            grad_mixed, w_down[...], (((1,), (1,)), ((), ())), preferred_element_type=F32
        )
        square = hidden * hidden
        gate = 0.5 + 0.5 * jnp.tanh(hidden * (root + (root * 0.044715) * square))
        act_f = hidden * gate
        slope = gate + act_f * (1.0 - gate) * (2.0 * root + (6.0 * root * 0.044715) * square)
        grad_pre_f = grad_act * slope
        activation = act_f.astype(BF)
        grad_pre = grad_pre_f.astype(BF)
        grad_scaled = lax.dot_general(
            grad_pre, w_up[...], (((1,), (1,)), ((), ())), preferred_element_type=F32
        )
        grad_normed = grad_scaled * ln_gain
        grad_conv_f = inverse * (
            grad_normed
            - jnp.mean(grad_normed, -1, keepdims=True)
            - normed * jnp.mean(grad_normed * normed, -1, keepdims=True)
        )
        grad_conv = grad_conv_f.astype(BF)
        for pair in range(PAIRS):
            upper = grad_conv[pair * extent : (pair + 1) * extent]
            lower = grad_conv[rows + pair * extent : rows + (pair + 1) * extent]
            grad_out[0, block * 2 * PAIRS + 2 * pair] = upper
            grad_out[0, block * 2 * PAIRS + 2 * pair + 1] = lower
        both = jnp.concatenate([grad_conv_f[:rows], grad_conv_f[rows:]], 1)
        grad_turned[block] = both.T.astype(BF)
        g_up[...] += lax.dot_general(
            scaled, grad_pre, (((0,), (0,)), ((), ())), preferred_element_type=F32
        )
        g_down[...] += lax.dot_general(
            grad_mixed, activation, (((0,), (0,)), ((), ())), preferred_element_type=F32
        )

        def fold(value):
            return jnp.sum(value.reshape(-1, 8, value.shape[1]), 0)

        g_vec[0] += fold(grad_conv_f)
        g_vec[1] += fold(grad_scaled * normed)
        g_vec[2] += fold(grad_scaled)
        g_vec[3] += fold(cot_rows)
        g_hidden[...] += fold(grad_pre_f)
        return carry

    blocks = extent // (2 * PAIRS)
    lax.fori_loop(0, blocks, block_step, 0)
    line = lax.broadcasted_iota(jnp.int32, (lanes, lanes), 0) % channels
    lane = lax.broadcasted_iota(jnp.int32, (lanes, lanes), 1) % channels

    for shift in range(7):

        def tap_step(step, carry, shift=shift):
            total = None
            for block in range(blocks):
                window = windows[shift, pl.ds(block * PAIRS + step, PAIRS)].reshape(rows, lanes)
                term = jnp.dot(grad_turned[block], window, preferred_element_type=F32)
                total = term if total is None else total + term
            diagonal = jnp.where(line == lane, total, jnp.zeros_like(total))
            even = jnp.sum(diagonal[:channels].reshape(-1, 8, lanes), 0)
            odd = jnp.sum(diagonal[channels:].reshape(-1, 8, lanes), 0)
            g_taps[0, shift * 4 + step] += even
            g_taps[1, shift * 4 + step] += odd
            return carry

        lax.fori_loop(0, 4, tap_step, 0)


def second_kernel(flags, tiles, cot, rv, rs, rc, taps, out, padded, windows):
    slot = pl.program_id(0)
    extent, channels = tiles.shape[1], tiles.shape[3]
    pairs = PAIRS
    build_windows(flags, slot, tiles, rv, rs, rc, padded, windows)
    keep = flags[slot, 8] > 0

    def block_step(block, carry):
        total = conv_block(windows, taps, block * pairs, pairs)
        for pair in range(pairs):
            for half in range(2):
                line = block * 2 * pairs + 2 * pair + half
                part = total[pair * extent : (pair + 1) * extent, half * channels : (half + 1) * channels]
                value = cot[0, line].astype(F32) + part
                out[0, line] = jnp.where(keep, value, jnp.zeros_like(value)).astype(BF)
        return carry

    lax.fori_loop(0, extent // (2 * pairs), block_step, 0)


def tap_matrices(kernel):
    channels = kernel.shape[2]
    by_column = jnp.transpose(kernel, (1, 0, 2)).astype(BF)
    padded = jnp.pad(by_column, ((0, 0), (1, 1), (0, 0)))
    to_even = padded[:, 1:9].reshape(7, 4, 2 * channels)
    to_odd = padded[:, 0:8].reshape(7, 4, 2 * channels)
    row = jnp.arange(2 * channels)
    lane = jnp.arange(2 * channels)
    same = (row[:, None] % channels) == (lane[None, :] % channels)
    values = jnp.where(
        lane[None, None, None, :] < channels, to_even[..., None], to_odd[..., None]
    )
    return jnp.where(same, values, jnp.zeros_like(values)).reshape(28, 2 * channels, 2 * channels)


def whole(shape):
    zeros = (0,) * len(shape)
    return pl.BlockSpec(shape, lambda i: zeros)


def local(
    fields,
    cotangent,
    is_ocean,
    neighbours,
    kernel,
    conv_bias,
    ln_gain,
    ln_bias,
    w_up,
    up_bias,
    w_down,
    down_bias,
    layer_scale,
):
    slots, extent, channels = fields.shape[1], fields.shape[2], fields.shape[4]
    hidden = w_up.shape[1]
    tile_count = lax.axis_size("tile")
    per_column = TROWS // slots
    position = lax.axis_index("tile")
    tiles, cot = fields[0], cotangent[0]

    ids = position * slots + jnp.arange(slots)
    column = ids // TROWS
    west_slot = 2 * TROWS * column - 1 - ids
    east_slot = 2 * TROWS * (column + 1) - 1 - ids
    expected = jnp.stack(
        [ids - 1, ids + 1, west_slot + 1, east_slot + 1, west_slot - 1, east_slot - 1], 1
    )
    upright = jnp.concatenate([neighbours[:, :2], neighbours[:, 4:]], 1)
    down = jnp.any((upright == expected) & (upright >= 0))
    flags = jnp.concatenate(
        [
            jnp.concatenate([(neighbours >= 0).astype(jnp.int32), is_ocean[:, None]], 1),
            jnp.broadcast_to(down.astype(jnp.int32), (1, 9)),
        ],
        0,
    )
    taps = tap_matrices(kernel)
    flipped_taps = tap_matrices(kernel[::-1, ::-1])
    vectors = jnp.stack([conv_bias, ln_gain, ln_bias, layer_scale], 0)

    rv, rs, rc = exchange(pack(tiles, down), per_column, 0)

    smem = pl.BlockSpec(memory_space=pltpu.SMEM)
    one_tile = pl.BlockSpec((1, extent, extent, channels), lambda i: (i, 0, 0, 0))
    padded_width = 16 + extent
    scratch = [
        pltpu.VMEM((extent + 6, padded_width, channels), F32),
        pltpu.VMEM((7, (extent + 6) // 2, extent, 2 * channels), BF),
    ]
    out_shapes = (
        jax.ShapeDtypeStruct(tiles.shape, BF),
        jax.ShapeDtypeStruct((2, 28, 8, 2 * channels), F32),
        jax.ShapeDtypeStruct((channels, hidden), F32),
        jax.ShapeDtypeStruct((channels, hidden), F32),
        jax.ShapeDtypeStruct((4, 8, channels), F32),
        jax.ShapeDtypeStruct((8, hidden), F32),
    )
    operands = (taps, vectors, w_up, up_bias[None], w_down)
    grad_tiles, g_taps, g_up, g_down, g_vec, g_hidden = pl.pallas_call(
        first_kernel,
        grid=(slots,),
        out_shape=out_shapes,
        in_specs=[smem, whole(tiles.shape), one_tile]
        + [whole(part.shape) for part in (rv, rs, rc) + operands],
        out_specs=(one_tile,) + tuple(whole(shape.shape) for shape in out_shapes[1:]),
        scratch_shapes=scratch
        + [pltpu.VMEM((extent // (2 * PAIRS), 2 * channels, PAIRS * extent), BF)],
        compiler_params=pltpu.CompilerParams(vmem_limit_bytes=VMEM_BYTES),
    )(flags, tiles, cot, rv, rs, rc, *operands)

    tap_sums = jnp.sum(g_taps, 2).reshape(2, 7, 8, channels)
    tap_sums = tap_sums[0, :, :7] + tap_sums[1, :, 1:]
    sums = lax.psum(
        (tap_sums, g_up, g_down, jnp.sum(g_vec, 1), jnp.sum(g_hidden, 0)), ("tile", "dp")
    )

    rv, rs, rc = exchange(pack(grad_tiles, down), per_column, 1)
    result = pl.pallas_call(
        second_kernel,
        grid=(slots,),
        out_shape=jax.ShapeDtypeStruct(tiles.shape, BF),
        in_specs=[smem, whole(tiles.shape), one_tile]
        + [whole(part.shape) for part in (rv, rs, rc, flipped_taps)],
        out_specs=one_tile,
        scratch_shapes=scratch,
        compiler_params=pltpu.CompilerParams(vmem_limit_bytes=VMEM_BYTES),
        cost_estimate=pl.CostEstimate(
            flops=2 * slots * extent * extent * 28 * channels * 2 * channels,
            bytes_accessed=8 * 1024 * 1024,
            transcendentals=0,
        ),
    )(flags, grad_tiles, cot, rv, rs, rc, flipped_taps)

    tap_sums, g_up, g_down, g_vec, g_hidden = sums
    scale = 1.0 / math.sqrt(
        fields.shape[0] * lax.axis_size("dp") * slots * tile_count * extent * extent
    )
    g_down = g_down.T
    g_scale = jnp.sum(w_down.astype(F32) * g_down, 0) / layer_scale + down_bias * g_vec[3]
    return (
        result[None],
        jnp.transpose(tap_sums, (1, 0, 2)) * scale,
        g_vec[0] * scale,
        g_vec[1] * scale,
        g_vec[2] * scale,
        g_up * scale,
        g_hidden * scale,
        g_down * scale,
        g_vec[3] * layer_scale * scale,
        g_scale * scale,
    )


def solution(mesh):
    tiled = P("dp", "tile", None, None, None)
    placed = (tiled, tiled, P("tile"), P("tile", None)) + (P(),) * 9
    return jax.shard_map(
        local,
        mesh=mesh,
        in_specs=placed,
        out_specs=(tiled,) + (P(),) * 9,
        check_vma=False,
    )
```

```python
from functools import partial
import math

import jax
import jax.numpy as jnp
from jax import lax
from jax.experimental import pallas as pl
from jax.experimental.pallas import tpu as pltpu
from jax.sharding import PartitionSpec as P

TROWS = 8
EPSILON = 1e-06
BF = jnp.bfloat16
F32 = jnp.float32
MESH = pl.DeviceIdType.MESH
PAIRS = 4
WEST = 5
VMEM_BYTES = 56 * 1024 * 1024


def halo_kernel(per_column, sv, ss, sc, rv, rs, rc, send_sems, recv_sems):
    tile_count = lax.axis_size("tile")
    me = lax.axis_index("tile")
    dp = lax.axis_index("dp")
    columns = tile_count // per_column
    col = me // per_column
    row = me % per_column
    mirror = per_column - 1 - row
    west = (col - 1) * per_column + mirror
    east = (col + 1) * per_column + mirror
    has_prev = row > 0
    has_next = row < per_column - 1
    has_west = col > 0
    has_east = col < columns - 1
    jobs = [
        (has_west, west, ss.at[0], rs.at[1], has_east),
        (has_east, east, ss.at[1], rs.at[0], has_west),
        (has_next, me + 1, sv.at[0], rv.at[0], has_prev),
        (has_prev, me - 1, sv.at[1], rv.at[1], has_next),
        (has_west & has_prev, west + 1, sc.at[0, 0], rc.at[1, 0], has_east & has_prev),
        (has_west & has_next, west - 1, sc.at[0, 1], rc.at[1, 1], has_east & has_next),
        (has_east & has_prev, east + 1, sc.at[1, 0], rc.at[0, 0], has_west & has_prev),
        (has_east & has_next, east - 1, sc.at[1, 1], rc.at[0, 1], has_west & has_next),
    ]
    barrier = pltpu.get_barrier_semaphore()
    for sends, target, _, _, _ in jobs:

        @pl.when(sends)
        def _(target=target):
            pl.semaphore_signal(barrier, inc=1, device_id=(target, dp), device_id_type=MESH)

    peers = sum(sends.astype(jnp.int32) for sends, _, _, _, _ in jobs)
    pl.semaphore_wait(barrier, peers)

    def copy_of(index):
        _, target, source, destination, _ = jobs[index]
        return pltpu.make_async_remote_copy(
            src_ref=source,
            dst_ref=destination,
            send_sem=send_sems.at[index],
            recv_sem=recv_sems.at[index],
            device_id=(target, dp),
            device_id_type=MESH,
        )

    for index in range(len(jobs)):

        @pl.when(jobs[index][0])
        def _(index=index):
            copy_of(index).start()

    for index in range(len(jobs)):

        @pl.when(jobs[index][4])
        def _(index=index):
            copy_of(index).wait_recv()

        @pl.when(jobs[index][0])
        def _(index=index):
            copy_of(index).wait_send()


def sum_kernel(steps, part, arrived, total, working, send_sems, recv_sems):
    position = {"tile": lax.axis_index("tile"), "dp": lax.axis_index("dp")}
    barrier = pltpu.get_barrier_semaphore()

    def partner(axis, stride):
        bit = (position[axis] // stride) % 2
        other = dict(position)
        other[axis] = position[axis] + stride - 2 * stride * bit
        return bit, (other["tile"], other["dp"])

    for axis, stride in steps:
        pl.semaphore_signal(
            barrier, inc=1, device_id=partner(axis, stride)[1], device_id_type=MESH
        )
    pl.semaphore_wait(barrier, len(steps))
    working[...] = part[...]
    length = part.shape[0]
    start = 0
    landing = 0
    held = []
    for index, (axis, stride) in enumerate(steps):
        bit, target = partner(axis, stride)
        length = length // 2
        mine = pl.multiple_of(start + bit * length, 8)
        given = pl.multiple_of(start + (1 - bit) * length, 8)
        copy = pltpu.make_async_remote_copy(
            src_ref=working.at[pl.ds(given, length)],
            dst_ref=arrived.at[pl.ds(landing, length)],
            send_sem=send_sems.at[index],
            recv_sem=recv_sems.at[index],
            device_id=target,
            device_id_type=MESH,
        )
        copy.start()
        copy.wait()
        working[pl.ds(mine, length)] = (
            working[pl.ds(mine, length)] + arrived[pl.ds(landing, length)]
        )
        held.append((mine, length, target))
        start = mine
        landing += length
    total[pl.ds(start, length)] = working[pl.ds(start, length)]
    for index in reversed(range(len(steps))):
        mine, length, target = held[index]
        copy = pltpu.make_async_remote_copy(
            src_ref=total.at[pl.ds(mine, length)],
            dst_ref=total.at[pl.ds(mine, length)],
            send_sem=send_sems.at[len(steps) + index],
            recv_sem=recv_sems.at[len(steps) + index],
            device_id=target,
            device_id_type=MESH,
        )
        copy.start()
        copy.wait()


def sum_over_devices(part, collective_id):
    steps = []
    for axis in ("dp", "tile"):
        stride = 1
        while stride < lax.axis_size(axis):
            steps.append((axis, stride))
            stride *= 2
    whole_rows = 8 * 2 ** len(steps)
    rows = -(-part.shape[0] // whole_rows) * whole_rows
    part = jnp.pad(part, ((0, rows - part.shape[0]), (0, 0)))
    shape = jax.ShapeDtypeStruct(part.shape, part.dtype)
    vmem = pl.BlockSpec(memory_space=pltpu.VMEM)
    return pl.pallas_call(
        lambda part, total, arrived, *rest: sum_kernel(steps, part, arrived, total, *rest),
        out_shape=shape,
        in_specs=[vmem],
        out_specs=vmem,
        scratch_shapes=[
            pltpu.VMEM(part.shape, part.dtype),
            pltpu.VMEM(part.shape, part.dtype),
            pltpu.SemaphoreType.DMA((2 * len(steps),)),
            pltpu.SemaphoreType.DMA((2 * len(steps),)),
        ],
        compiler_params=pltpu.CompilerParams(
            collective_id=collective_id, has_side_effects=True, vmem_limit_bytes=16 * 1024 * 1024
        ),
    )(part)


def exchange(packed, per_column, collective_id):
    any_spec = pl.BlockSpec(memory_space=pl.ANY)
    return pl.pallas_call(
        partial(halo_kernel, per_column),
        out_shape=tuple(jax.ShapeDtypeStruct(part.shape, part.dtype) for part in packed),
        in_specs=[any_spec] * 3,
        out_specs=(any_spec,) * 3,
        scratch_shapes=[pltpu.SemaphoreType.DMA((8,)), pltpu.SemaphoreType.DMA((8,))],
        compiler_params=pltpu.CompilerParams(collective_id=collective_id, has_side_effects=True),
    )(*packed)


def pack(tiles, down):
    extent = tiles.shape[1]
    first, last = tiles[0], tiles[1]
    to_next = jnp.where(down, last[extent - 3 :], last[:3])
    to_prev = jnp.where(down, first[:3], first[extent - 3 :])
    vertical = jnp.stack([to_next, to_prev], 0)
    west = jnp.transpose(tiles[:, :, :3], (0, 2, 1, 3))
    east = jnp.transpose(tiles[:, :, extent - 3 :], (0, 2, 1, 3))
    sides = jnp.stack([west, east], 0)
    low, high = sides[:, :, :, :16], sides[:, :, :, extent - 16 :]
    corner_prev = jnp.where(down, low[:, 0], high[:, 0])
    corner_next = jnp.where(down, high[:, 1], low[:, 1])
    return vertical, sides, jnp.stack([corner_prev, corner_next], 1)


def build_windows(flags, slot, tiles, rv, rs, rc, padded, windows):
    extent = tiles.shape[1]
    width = padded.shape[1]
    down = flags[2, 0] > 0
    first = slot == 0

    def valid(direction, value):
        return jnp.where(flags[slot, direction] > 0, value, jnp.zeros_like(value))

    own = tiles.at[slot]
    other = tiles.at[1 - slot]
    padded[3 : 3 + extent, 8 : 8 + extent, :] = own[...].astype(F32)
    outer = rv[slot].astype(F32)
    inner_is_south = first == down
    inner = jnp.where(inner_is_south, other[:3], other[extent - 3 :]).astype(F32)
    north = jnp.where(inner_is_south, outer, inner)
    south = jnp.where(inner_is_south, inner, outer)
    padded[0:3, 8 : 8 + extent, :] = valid(0, north)
    padded[3 + extent : 6 + extent, 8 : 8 + extent, :] = valid(1, south)
    flat = padded.reshape(padded.shape[0] * width, padded.shape[2])
    for side, base, straight, upper, lower in ((0, WEST, 2, 4, 6), (1, 8 + extent, 3, 5, 7)):
        strips = valid(straight, rs[side, 1 - slot].astype(F32))
        inner_strips = rs[side, slot].astype(F32)
        corner = rc[side, slot].astype(F32)
        above = valid(upper, jnp.where(inner_is_south, corner[:, 13:16], inner_strips[:, extent - 3 :]))
        below = valid(lower, jnp.where(inner_is_south, inner_strips[:, :3], corner[:, 0:3]))
        for column in range(3):
            flat[pl.ds(3 * width + base + column, extent, stride=width), :] = strips[column]
            for line in range(3):
                padded[line, base + column : base + column + 1, :] = above[column, line : line + 1]
                padded[3 + extent + line, base + column : base + column + 1, :] = below[
                    column, line : line + 1
                ]

    def fill(pair, carry):
        for shift in range(7):
            upper_row = padded[2 * pair, WEST + shift : WEST + shift + extent, :]
            lower_row = padded[2 * pair + 1, WEST + shift : WEST + shift + extent, :]
            windows[shift, pair] = jnp.concatenate([upper_row, lower_row], 1).astype(BF)
        return carry

    lax.fori_loop(0, (extent + 6) // 2, fill, 0)


def conv_block(windows, taps, first_pair, pairs):
    extent, lanes = windows.shape[2], windows.shape[3]
    total = None
    for shift in range(7):
        for step in range(4):
            rows = windows[shift, pl.ds(first_pair + step, pairs)].reshape(pairs * extent, lanes)
            term = jnp.dot(rows, taps[shift * 4 + step], preferred_element_type=F32)
            total = term if total is None else total + term
    return total


def split_rows(block):
    pairs = block.shape[0] // 2
    parts = [block[2 * q] for q in range(pairs)] + [block[2 * q + 1] for q in range(pairs)]
    return jnp.concatenate(parts, 0)


def first_kernel(
    flags,
    tiles,
    cot,
    rv,
    rs,
    rc,
    taps,
    vectors,
    w_up,
    up_bias,
    w_down,
    grad_out,
    g_taps,
    g_up,
    g_down,
    g_vec,
    g_hidden,
    padded,
    windows,
    grad_turned,
):
    slot = pl.program_id(0)
    extent, channels = tiles.shape[1], tiles.shape[3]
    lanes = 2 * channels
    rows = PAIRS * extent

    @pl.when(slot == 0)
    def _():
        g_taps[...] = jnp.zeros_like(g_taps)
        g_up[...] = jnp.zeros_like(g_up)
        g_down[...] = jnp.zeros_like(g_down)
        g_vec[...] = jnp.zeros_like(g_vec)
        g_hidden[...] = jnp.zeros_like(g_hidden)

    build_windows(flags, slot, tiles, rv, rs, rc, padded, windows)
    keep = flags[slot, 8] > 0
    conv_bias, ln_gain, ln_bias, layer_scale = (vectors[k : k + 1] for k in range(4))
    root = math.sqrt(2.0 / math.pi)

    def block_step(block, carry):
        total = conv_block(windows, taps, block * PAIRS, PAIRS)
        conv = jnp.concatenate([total[:, :channels], total[:, channels:]], 0) + conv_bias
        cot_rows = split_rows(cot[0, pl.ds(block * 2 * PAIRS, 2 * PAIRS)]).astype(F32)
        cot_rows = jnp.where(keep, cot_rows, jnp.zeros_like(cot_rows))
        centred = conv - jnp.mean(conv, -1, keepdims=True)
        inverse = lax.rsqrt(jnp.mean(centred * centred, -1, keepdims=True) + EPSILON)
        normed = centred * inverse
        scaled = (normed * ln_gain + ln_bias).astype(BF)
        hidden = jnp.dot(scaled, w_up[...], preferred_element_type=F32) + up_bias[...]
        grad_mixed_f = cot_rows * layer_scale
        grad_mixed = grad_mixed_f.astype(BF)
        grad_act = lax.dot_general(
            grad_mixed, w_down[...], (((1,), (1,)), ((), ())), preferred_element_type=F32
        )
        square = hidden * hidden
        gate = 0.5 + 0.5 * jnp.tanh(hidden * (root + (root * 0.044715) * square))
        act_f = hidden * gate
        slope = gate + act_f * (1.0 - gate) * (2.0 * root + (6.0 * root * 0.044715) * square)
        grad_pre_f = grad_act * slope
        activation = act_f.astype(BF)
        grad_pre = grad_pre_f.astype(BF)
        grad_scaled = lax.dot_general(
            grad_pre, w_up[...], (((1,), (1,)), ((), ())), preferred_element_type=F32
        )
        grad_normed = grad_scaled * ln_gain
        grad_conv_f = inverse * (
            grad_normed
            - jnp.mean(grad_normed, -1, keepdims=True)
            - normed * jnp.mean(grad_normed * normed, -1, keepdims=True)
        )
        grad_conv = grad_conv_f.astype(BF)
        for pair in range(PAIRS):
            upper = grad_conv[pair * extent : (pair + 1) * extent]
            lower = grad_conv[rows + pair * extent : rows + (pair + 1) * extent]
            grad_out[0, block * 2 * PAIRS + 2 * pair] = upper
            grad_out[0, block * 2 * PAIRS + 2 * pair + 1] = lower
        both = jnp.concatenate([grad_conv_f[:rows], grad_conv_f[rows:]], 1)
        grad_turned[block] = both.T.astype(BF)
        g_up[...] += lax.dot_general(
            scaled, grad_pre, (((0,), (0,)), ((), ())), preferred_element_type=F32
        )
        g_down[...] += lax.dot_general(
            grad_mixed, activation, (((0,), (0,)), ((), ())), preferred_element_type=F32
        )

        def fold(value):
            return jnp.sum(value.reshape(-1, 8, value.shape[1]), 0)

        g_vec[0] += fold(grad_conv_f)
        g_vec[1] += fold(grad_scaled * normed)
        g_vec[2] += fold(grad_scaled)
        g_vec[3] += fold(cot_rows)
        g_hidden[...] += fold(grad_pre_f)
        return carry

    blocks = extent // (2 * PAIRS)
    lax.fori_loop(0, blocks, block_step, 0)
    line = lax.broadcasted_iota(jnp.int32, (lanes, lanes), 0) % channels
    lane = lax.broadcasted_iota(jnp.int32, (lanes, lanes), 1) % channels

    for shift in range(7):

        def tap_step(step, carry, shift=shift):
            total = None
            for block in range(blocks):
                window = windows[shift, pl.ds(block * PAIRS + step, PAIRS)].reshape(rows, lanes)
                term = jnp.dot(grad_turned[block], window, preferred_element_type=F32)
                total = term if total is None else total + term
            diagonal = jnp.where(line == lane, total, jnp.zeros_like(total))
            even = jnp.sum(diagonal[:channels].reshape(-1, 8, lanes), 0)
            odd = jnp.sum(diagonal[channels:].reshape(-1, 8, lanes), 0)
            g_taps[0, shift * 4 + step] += even
            g_taps[1, shift * 4 + step] += odd
            return carry

        lax.fori_loop(0, 4, tap_step, 0)


def second_kernel(flags, tiles, cot, rv, rs, rc, taps, out, padded, windows):
    slot = pl.program_id(0)
    extent, channels = tiles.shape[1], tiles.shape[3]
    pairs = PAIRS
    build_windows(flags, slot, tiles, rv, rs, rc, padded, windows)
    keep = flags[slot, 8] > 0

    def block_step(block, carry):
        total = conv_block(windows, taps, block * pairs, pairs)
        for pair in range(pairs):
            for half in range(2):
                line = block * 2 * pairs + 2 * pair + half
                part = total[pair * extent : (pair + 1) * extent, half * channels : (half + 1) * channels]
                value = cot[0, line].astype(F32) + part
                out[0, line] = jnp.where(keep, value, jnp.zeros_like(value)).astype(BF)
        return carry

    lax.fori_loop(0, extent // (2 * pairs), block_step, 0)


def tap_matrices(kernel):
    channels = kernel.shape[2]
    by_column = jnp.transpose(kernel, (1, 0, 2)).astype(BF)
    padded = jnp.pad(by_column, ((0, 0), (1, 1), (0, 0)))
    to_even = padded[:, 1:9].reshape(7, 4, 2 * channels)
    to_odd = padded[:, 0:8].reshape(7, 4, 2 * channels)
    row = jnp.arange(2 * channels)
    lane = jnp.arange(2 * channels)
    same = (row[:, None] % channels) == (lane[None, :] % channels)
    values = jnp.where(
        lane[None, None, None, :] < channels, to_even[..., None], to_odd[..., None]
    )
    return jnp.where(same, values, jnp.zeros_like(values)).reshape(28, 2 * channels, 2 * channels)


def whole(shape):
    zeros = (0,) * len(shape)
    return pl.BlockSpec(shape, lambda i: zeros)


def local(
    fields,
    cotangent,
    is_ocean,
    neighbours,
    kernel,
    conv_bias,
    ln_gain,
    ln_bias,
    w_up,
    up_bias,
    w_down,
    down_bias,
    layer_scale,
):
    slots, extent, channels = fields.shape[1], fields.shape[2], fields.shape[4]
    hidden = w_up.shape[1]
    tile_count = lax.axis_size("tile")
    per_column = TROWS // slots
    position = lax.axis_index("tile")
    tiles, cot = fields[0], cotangent[0]

    ids = position * slots + jnp.arange(slots)
    column = ids // TROWS
    west_slot = 2 * TROWS * column - 1 - ids
    east_slot = 2 * TROWS * (column + 1) - 1 - ids
    expected = jnp.stack(
        [ids - 1, ids + 1, west_slot + 1, east_slot + 1, west_slot - 1, east_slot - 1], 1
    )
    upright = jnp.concatenate([neighbours[:, :2], neighbours[:, 4:]], 1)
    down = jnp.any((upright == expected) & (upright >= 0))
    flags = jnp.concatenate(
        [
            jnp.concatenate([(neighbours >= 0).astype(jnp.int32), is_ocean[:, None]], 1),
            jnp.broadcast_to(down.astype(jnp.int32), (1, 9)),
        ],
        0,
    )
    taps = tap_matrices(kernel)
    flipped_taps = tap_matrices(kernel[::-1, ::-1])
    vectors = jnp.stack([conv_bias, ln_gain, ln_bias, layer_scale], 0)

    rv, rs, rc = exchange(pack(tiles, down), per_column, 0)

    smem = pl.BlockSpec(memory_space=pltpu.SMEM)
    one_tile = pl.BlockSpec((1, extent, extent, channels), lambda i: (i, 0, 0, 0))
    padded_width = 16 + extent
    scratch = [
        pltpu.VMEM((extent + 6, padded_width, channels), F32),
        pltpu.VMEM((7, (extent + 6) // 2, extent, 2 * channels), BF),
    ]
    out_shapes = (
        jax.ShapeDtypeStruct(tiles.shape, BF),
        jax.ShapeDtypeStruct((2, 28, 8, 2 * channels), F32),
        jax.ShapeDtypeStruct((channels, hidden), F32),
        jax.ShapeDtypeStruct((channels, hidden), F32),
        jax.ShapeDtypeStruct((4, 8, channels), F32),
        jax.ShapeDtypeStruct((8, hidden), F32),
    )
    operands = (taps, vectors, w_up, up_bias[None], w_down)
    grad_tiles, g_taps, g_up, g_down, g_vec, g_hidden = pl.pallas_call(
        first_kernel,
        grid=(slots,),
        out_shape=out_shapes,
        in_specs=[smem, whole(tiles.shape), one_tile]
        + [whole(part.shape) for part in (rv, rs, rc) + operands],
        out_specs=(one_tile,) + tuple(whole(shape.shape) for shape in out_shapes[1:]),
        scratch_shapes=scratch
        + [pltpu.VMEM((extent // (2 * PAIRS), 2 * channels, PAIRS * extent), BF)],
        compiler_params=pltpu.CompilerParams(vmem_limit_bytes=VMEM_BYTES),
    )(flags, tiles, cot, rv, rs, rc, *operands)

    tap_sums = jnp.sum(g_taps, 2).reshape(2, 7, 8, channels)
    tap_sums = tap_sums[0, :, :7] + tap_sums[1, :, 1:]
    strips = hidden // channels

    def stacked(matrix):
        return jnp.concatenate(
            [matrix[:, k * channels : (k + 1) * channels] for k in range(strips)], 0
        )

    def unstacked(rows):
        return jnp.concatenate(jnp.split(rows, strips, 0), 1)

    parts = [
        stacked(g_up),
        stacked(g_down),
        tap_sums.reshape(49, channels),
        jnp.sum(g_vec, 1),
        stacked(jnp.sum(g_hidden, 0)[None]),
    ]
    rv, rs, rc = exchange(pack(grad_tiles, down), per_column, 1)
    result = pl.pallas_call(
        second_kernel,
        grid=(slots,),
        out_shape=jax.ShapeDtypeStruct(tiles.shape, BF),
        in_specs=[smem, whole(tiles.shape), one_tile]
        + [whole(part.shape) for part in (rv, rs, rc, flipped_taps)],
        out_specs=one_tile,
        scratch_shapes=scratch,
        compiler_params=pltpu.CompilerParams(vmem_limit_bytes=VMEM_BYTES),
        cost_estimate=pl.CostEstimate(
            flops=2 * slots * extent * extent * 28 * channels * 2 * channels,
            bytes_accessed=8 * 1024 * 1024,
            transcendentals=0,
        ),
    )(flags, grad_tiles, cot, rv, rs, rc, flipped_taps)

    sums = sum_over_devices(jnp.concatenate(parts, 0), 2)
    pieces = []
    first = 0
    for part in parts:
        pieces.append(sums[first : first + part.shape[0]])
        first += part.shape[0]
    g_up, g_down = unstacked(pieces[0]), unstacked(pieces[1])
    tap_sums = pieces[2].reshape(7, 7, channels)
    g_vec = pieces[3]
    g_hidden = unstacked(pieces[4])[0]
    scale = 1.0 / math.sqrt(
        fields.shape[0] * lax.axis_size("dp") * slots * tile_count * extent * extent
    )
    g_down = g_down.T
    g_scale = jnp.sum(w_down.astype(F32) * g_down, 0) / layer_scale + down_bias * g_vec[3]
    return (
        result[None],
        jnp.transpose(tap_sums, (1, 0, 2)) * scale,
        g_vec[0] * scale,
        g_vec[1] * scale,
        g_vec[2] * scale,
        g_up * scale,
        g_hidden * scale,
        g_down * scale,
        g_vec[3] * layer_scale * scale,
        g_scale * scale,
    )


def solution(mesh):
    tiled = P("dp", "tile", None, None, None)
    placed = (tiled, tiled, P("tile"), P("tile", None)) + (P(),) * 9
    return jax.shard_map(
        local,
        mesh=mesh,
        in_specs=placed,
        out_specs=(tiled,) + (P(),) * 9,
        check_vma=False,
    )
```

```python
from functools import partial
import math

import jax
import jax.numpy as jnp
from jax import lax
from jax.experimental import pallas as pl
from jax.experimental.pallas import tpu as pltpu
from jax.sharding import PartitionSpec as P

TROWS = 8
EPSILON = 1e-06
BF = jnp.bfloat16
F32 = jnp.float32
MESH = pl.DeviceIdType.MESH
PAIRS = 8
WEST = 5
VMEM_BYTES = 56 * 1024 * 1024


def halo_kernel(per_column, sv, ss, sc, rv, rs, rc, send_sems, recv_sems):
    tile_count = lax.axis_size("tile")
    me = lax.axis_index("tile")
    dp = lax.axis_index("dp")
    columns = tile_count // per_column
    col = me // per_column
    row = me % per_column
    mirror = per_column - 1 - row
    west = (col - 1) * per_column + mirror
    east = (col + 1) * per_column + mirror
    has_prev = row > 0
    has_next = row < per_column - 1
    has_west = col > 0
    has_east = col < columns - 1
    jobs = [
        (has_west, west, ss.at[0], rs.at[1], has_east),
        (has_east, east, ss.at[1], rs.at[0], has_west),
        (has_next, me + 1, sv.at[0], rv.at[0], has_prev),
        (has_prev, me - 1, sv.at[1], rv.at[1], has_next),
        (has_west & has_prev, west + 1, sc.at[0, 0], rc.at[1, 0], has_east & has_prev),
        (has_west & has_next, west - 1, sc.at[0, 1], rc.at[1, 1], has_east & has_next),
        (has_east & has_prev, east + 1, sc.at[1, 0], rc.at[0, 0], has_west & has_prev),
        (has_east & has_next, east - 1, sc.at[1, 1], rc.at[0, 1], has_west & has_next),
    ]
    barrier = pltpu.get_barrier_semaphore()
    for sends, target, _, _, _ in jobs:

        @pl.when(sends)
        def _(target=target):
            pl.semaphore_signal(barrier, inc=1, device_id=(target, dp), device_id_type=MESH)

    peers = sum(sends.astype(jnp.int32) for sends, _, _, _, _ in jobs)
    pl.semaphore_wait(barrier, peers)

    def copy_of(index):
        _, target, source, destination, _ = jobs[index]
        return pltpu.make_async_remote_copy(
            src_ref=source,
            dst_ref=destination,
            send_sem=send_sems.at[index],
            recv_sem=recv_sems.at[index],
            device_id=(target, dp),
            device_id_type=MESH,
        )

    for index in range(len(jobs)):

        @pl.when(jobs[index][0])
        def _(index=index):
            copy_of(index).start()

    for index in range(len(jobs)):

        @pl.when(jobs[index][4])
        def _(index=index):
            copy_of(index).wait_recv()

        @pl.when(jobs[index][0])
        def _(index=index):
            copy_of(index).wait_send()


def sum_kernel(steps, part, arrived, total, working, send_sems, recv_sems):
    position = {"tile": lax.axis_index("tile"), "dp": lax.axis_index("dp")}
    barrier = pltpu.get_barrier_semaphore()

    def partner(axis, stride):
        bit = (position[axis] // stride) % 2
        other = dict(position)
        other[axis] = position[axis] + stride - 2 * stride * bit
        return bit, (other["tile"], other["dp"])

    for axis, stride in steps:
        pl.semaphore_signal(
            barrier, inc=1, device_id=partner(axis, stride)[1], device_id_type=MESH
        )
    pl.semaphore_wait(barrier, len(steps))
    working[...] = part[...]
    length = part.shape[0]
    start = 0
    landing = 0
    held = []
    for index, (axis, stride) in enumerate(steps):
        bit, target = partner(axis, stride)
        length = length // 2
        mine = pl.multiple_of(start + bit * length, 8)
        given = pl.multiple_of(start + (1 - bit) * length, 8)
        copy = pltpu.make_async_remote_copy(
            src_ref=working.at[pl.ds(given, length)],
            dst_ref=arrived.at[pl.ds(landing, length)],
            send_sem=send_sems.at[index],
            recv_sem=recv_sems.at[index],
            device_id=target,
            device_id_type=MESH,
        )
        copy.start()
        copy.wait()
        working[pl.ds(mine, length)] = (
            working[pl.ds(mine, length)] + arrived[pl.ds(landing, length)]
        )
        held.append((mine, length, target))
        start = mine
        landing += length
    total[pl.ds(start, length)] = working[pl.ds(start, length)]
    for index in reversed(range(len(steps))):
        mine, length, target = held[index]
        copy = pltpu.make_async_remote_copy(
            src_ref=total.at[pl.ds(mine, length)],
            dst_ref=total.at[pl.ds(mine, length)],
            send_sem=send_sems.at[len(steps) + index],
            recv_sem=recv_sems.at[len(steps) + index],
            device_id=target,
            device_id_type=MESH,
        )
        copy.start()
        copy.wait()


def sum_over_devices(part, collective_id):
    steps = []
    for axis in ("dp", "tile"):
        stride = 1
        while stride < lax.axis_size(axis):
            steps.append((axis, stride))
            stride *= 2
    whole_rows = 8 * 2 ** len(steps)
    rows = -(-part.shape[0] // whole_rows) * whole_rows
    part = jnp.pad(part, ((0, rows - part.shape[0]), (0, 0)))
    shape = jax.ShapeDtypeStruct(part.shape, part.dtype)
    vmem = pl.BlockSpec(memory_space=pltpu.VMEM)
    return pl.pallas_call(
        lambda part, total, arrived, *rest: sum_kernel(steps, part, arrived, total, *rest),
        out_shape=shape,
        in_specs=[vmem],
        out_specs=vmem,
        scratch_shapes=[
            pltpu.VMEM(part.shape, part.dtype),
            pltpu.VMEM(part.shape, part.dtype),
            pltpu.SemaphoreType.DMA((2 * len(steps),)),
            pltpu.SemaphoreType.DMA((2 * len(steps),)),
        ],
        compiler_params=pltpu.CompilerParams(
            collective_id=collective_id, has_side_effects=True, vmem_limit_bytes=16 * 1024 * 1024
        ),
    )(part)


def exchange(packed, per_column, collective_id):
    any_spec = pl.BlockSpec(memory_space=pl.ANY)
    return pl.pallas_call(
        partial(halo_kernel, per_column),
        out_shape=tuple(jax.ShapeDtypeStruct(part.shape, part.dtype) for part in packed),
        in_specs=[any_spec] * 3,
        out_specs=(any_spec,) * 3,
        scratch_shapes=[pltpu.SemaphoreType.DMA((8,)), pltpu.SemaphoreType.DMA((8,))],
        compiler_params=pltpu.CompilerParams(collective_id=collective_id, has_side_effects=True),
    )(*packed)


def pack(tiles, down):
    extent = tiles.shape[1]
    first, last = tiles[0], tiles[1]
    to_next = jnp.where(down, last[extent - 3 :], last[:3])
    to_prev = jnp.where(down, first[:3], first[extent - 3 :])
    vertical = jnp.stack([to_next, to_prev], 0)
    west = jnp.transpose(tiles[:, :, :3], (0, 2, 1, 3))
    east = jnp.transpose(tiles[:, :, extent - 3 :], (0, 2, 1, 3))
    sides = jnp.stack([west, east], 0)
    low, high = sides[:, :, :, :16], sides[:, :, :, extent - 16 :]
    corner_prev = jnp.where(down, low[:, 0], high[:, 0])
    corner_next = jnp.where(down, high[:, 1], low[:, 1])
    return vertical, sides, jnp.stack([corner_prev, corner_next], 1)


def build_windows(flags, slot, tiles, rv, rs, rc, padded, windows):
    extent = tiles.shape[1]
    width = padded.shape[1]
    down = flags[2, 0] > 0
    first = slot == 0

    def valid(direction, value):
        return jnp.where(flags[slot, direction] > 0, value, jnp.zeros_like(value))

    own = tiles.at[slot]
    other = tiles.at[1 - slot]
    padded[3 : 3 + extent, 8 : 8 + extent, :] = own[...].astype(F32)
    outer = rv[slot].astype(F32)
    inner_is_south = first == down
    inner = jnp.where(inner_is_south, other[:3], other[extent - 3 :]).astype(F32)
    north = jnp.where(inner_is_south, outer, inner)
    south = jnp.where(inner_is_south, inner, outer)
    padded[0:3, 8 : 8 + extent, :] = valid(0, north)
    padded[3 + extent : 6 + extent, 8 : 8 + extent, :] = valid(1, south)
    flat = padded.reshape(padded.shape[0] * width, padded.shape[2])
    for side, base, straight, upper, lower in ((0, WEST, 2, 4, 6), (1, 8 + extent, 3, 5, 7)):
        strips = valid(straight, rs[side, 1 - slot].astype(F32))
        inner_strips = rs[side, slot].astype(F32)
        corner = rc[side, slot].astype(F32)
        above = valid(upper, jnp.where(inner_is_south, corner[:, 13:16], inner_strips[:, extent - 3 :]))
        below = valid(lower, jnp.where(inner_is_south, inner_strips[:, :3], corner[:, 0:3]))
        for column in range(3):
            flat[pl.ds(3 * width + base + column, extent, stride=width), :] = strips[column]
            for line in range(3):
                padded[line, base + column : base + column + 1, :] = above[column, line : line + 1]
                padded[3 + extent + line, base + column : base + column + 1, :] = below[
                    column, line : line + 1
                ]

    def fill(pair, carry):
        for shift in range(7):
            upper_row = padded[2 * pair, WEST + shift : WEST + shift + extent, :]
            lower_row = padded[2 * pair + 1, WEST + shift : WEST + shift + extent, :]
            windows[shift, pair] = jnp.concatenate([upper_row, lower_row], 1).astype(BF)
        return carry

    lax.fori_loop(0, (extent + 6) // 2, fill, 0)


def conv_block(windows, taps, first_pair, pairs):
    extent, lanes = windows.shape[2], windows.shape[3]
    total = None
    for shift in range(7):
        for step in range(4):
            rows = windows[shift, pl.ds(first_pair + step, pairs)].reshape(pairs * extent, lanes)
            term = jnp.dot(rows, taps[shift * 4 + step], preferred_element_type=F32)
            total = term if total is None else total + term
    return total


def split_rows(block):
    pairs = block.shape[0] // 2
    parts = [block[2 * q] for q in range(pairs)] + [block[2 * q + 1] for q in range(pairs)]
    return jnp.concatenate(parts, 0)


def first_kernel(
    flags,
    tiles,
    cot,
    rv,
    rs,
    rc,
    taps,
    vectors,
    w_up,
    up_bias,
    w_down,
    grad_out,
    g_taps,
    g_up,
    g_down,
    g_vec,
    g_hidden,
    padded,
    windows,
    grad_turned,
):
    slot = pl.program_id(0)
    extent, channels = tiles.shape[1], tiles.shape[3]
    lanes = 2 * channels
    rows = PAIRS * extent

    @pl.when(slot == 0)
    def _():
        g_taps[...] = jnp.zeros_like(g_taps)
        g_up[...] = jnp.zeros_like(g_up)
        g_down[...] = jnp.zeros_like(g_down)
        g_vec[...] = jnp.zeros_like(g_vec)
        g_hidden[...] = jnp.zeros_like(g_hidden)

    build_windows(flags, slot, tiles, rv, rs, rc, padded, windows)
    keep = flags[slot, 8] > 0
    conv_bias, ln_gain, ln_bias, layer_scale = (vectors[k : k + 1] for k in range(4))
    root = math.sqrt(2.0 / math.pi)

    def block_step(block, carry):
        total = conv_block(windows, taps, block * PAIRS, PAIRS)
        conv = jnp.concatenate([total[:, :channels], total[:, channels:]], 0) + conv_bias
        cot_rows = split_rows(cot[0, pl.ds(block * 2 * PAIRS, 2 * PAIRS)]).astype(F32)
        cot_rows = jnp.where(keep, cot_rows, jnp.zeros_like(cot_rows))
        centred = conv - jnp.mean(conv, -1, keepdims=True)
        inverse = lax.rsqrt(jnp.mean(centred * centred, -1, keepdims=True) + EPSILON)
        normed = centred * inverse
        scaled = (normed * ln_gain + ln_bias).astype(BF)
        hidden = jnp.dot(scaled, w_up[...], preferred_element_type=F32) + up_bias[...]
        grad_mixed_f = cot_rows * layer_scale
        grad_mixed = grad_mixed_f.astype(BF)
        grad_act = lax.dot_general(
            grad_mixed, w_down[...], (((1,), (1,)), ((), ())), preferred_element_type=F32
        )
        square = hidden * hidden
        gate = 0.5 + 0.5 * jnp.tanh(hidden * (root + (root * 0.044715) * square))
        act_f = hidden * gate
        slope = gate + act_f * (1.0 - gate) * (2.0 * root + (6.0 * root * 0.044715) * square)
        grad_pre_f = grad_act * slope
        activation = act_f.astype(BF)
        grad_pre = grad_pre_f.astype(BF)
        grad_scaled = lax.dot_general(
            grad_pre, w_up[...], (((1,), (1,)), ((), ())), preferred_element_type=F32
        )
        grad_normed = grad_scaled * ln_gain
        grad_conv_f = inverse * (
            grad_normed
            - jnp.mean(grad_normed, -1, keepdims=True)
            - normed * jnp.mean(grad_normed * normed, -1, keepdims=True)
        )
        grad_conv = grad_conv_f.astype(BF)
        for pair in range(PAIRS):
            upper = grad_conv[pair * extent : (pair + 1) * extent]
            lower = grad_conv[rows + pair * extent : rows + (pair + 1) * extent]
            grad_out[0, block * 2 * PAIRS + 2 * pair] = upper
            grad_out[0, block * 2 * PAIRS + 2 * pair + 1] = lower
        both = jnp.concatenate([grad_conv_f[:rows], grad_conv_f[rows:]], 1)
        grad_turned[block] = both.T.astype(BF)
        g_up[...] += lax.dot_general(
            scaled, grad_pre, (((0,), (0,)), ((), ())), preferred_element_type=F32
        )
        g_down[...] += lax.dot_general(
            grad_mixed, activation, (((0,), (0,)), ((), ())), preferred_element_type=F32
        )

        def fold(value):
            return jnp.sum(value.reshape(-1, 8, value.shape[1]), 0)

        g_vec[0] += fold(grad_conv_f)
        g_vec[1] += fold(grad_scaled * normed)
        g_vec[2] += fold(grad_scaled)
        g_vec[3] += fold(cot_rows)
        g_hidden[...] += fold(grad_pre_f)
        return carry

    blocks = extent // (2 * PAIRS)
    lax.fori_loop(0, blocks, block_step, 0)
    line = lax.broadcasted_iota(jnp.int32, (lanes, lanes), 0) % channels
    lane = lax.broadcasted_iota(jnp.int32, (lanes, lanes), 1) % channels

    for shift in range(7):

        def tap_step(step, carry, shift=shift):
            total = None
            for block in range(blocks):
                window = windows[shift, pl.ds(block * PAIRS + step, PAIRS)].reshape(rows, lanes)
                term = jnp.dot(grad_turned[block], window, preferred_element_type=F32)
                total = term if total is None else total + term
            diagonal = jnp.where(line == lane, total, jnp.zeros_like(total))
            even = jnp.sum(diagonal[:channels].reshape(-1, 8, lanes), 0)
            odd = jnp.sum(diagonal[channels:].reshape(-1, 8, lanes), 0)
            g_taps[0, shift * 4 + step] += even
            g_taps[1, shift * 4 + step] += odd
            return carry

        lax.fori_loop(0, 4, tap_step, 0)


def second_kernel(flags, tiles, cot, rv, rs, rc, taps, out, padded, windows):
    slot = pl.program_id(0)
    extent, channels = tiles.shape[1], tiles.shape[3]
    pairs = PAIRS
    build_windows(flags, slot, tiles, rv, rs, rc, padded, windows)
    keep = flags[slot, 8] > 0

    def block_step(block, carry):
        total = conv_block(windows, taps, block * pairs, pairs)
        for pair in range(pairs):
            for half in range(2):
                line = block * 2 * pairs + 2 * pair + half
                part = total[pair * extent : (pair + 1) * extent, half * channels : (half + 1) * channels]
                value = cot[0, line].astype(F32) + part
                out[0, line] = jnp.where(keep, value, jnp.zeros_like(value)).astype(BF)
        return carry

    lax.fori_loop(0, extent // (2 * pairs), block_step, 0)


def tap_matrices(kernel):
    channels = kernel.shape[2]
    by_column = jnp.transpose(kernel, (1, 0, 2)).astype(BF)
    padded = jnp.pad(by_column, ((0, 0), (1, 1), (0, 0)))
    to_even = padded[:, 1:9].reshape(7, 4, 2 * channels)
    to_odd = padded[:, 0:8].reshape(7, 4, 2 * channels)
    row = jnp.arange(2 * channels)
    lane = jnp.arange(2 * channels)
    same = (row[:, None] % channels) == (lane[None, :] % channels)
    values = jnp.where(
        lane[None, None, None, :] < channels, to_even[..., None], to_odd[..., None]
    )
    return jnp.where(same, values, jnp.zeros_like(values)).reshape(28, 2 * channels, 2 * channels)


def whole(shape):
    zeros = (0,) * len(shape)
    return pl.BlockSpec(shape, lambda i: zeros)


def local(
    fields,
    cotangent,
    is_ocean,
    neighbours,
    kernel,
    conv_bias,
    ln_gain,
    ln_bias,
    w_up,
    up_bias,
    w_down,
    down_bias,
    layer_scale,
):
    slots, extent, channels = fields.shape[1], fields.shape[2], fields.shape[4]
    hidden = w_up.shape[1]
    tile_count = lax.axis_size("tile")
    per_column = TROWS // slots
    position = lax.axis_index("tile")
    tiles, cot = fields[0], cotangent[0]

    ids = position * slots + jnp.arange(slots)
    column = ids // TROWS
    west_slot = 2 * TROWS * column - 1 - ids
    east_slot = 2 * TROWS * (column + 1) - 1 - ids
    expected = jnp.stack(
        [ids - 1, ids + 1, west_slot + 1, east_slot + 1, west_slot - 1, east_slot - 1], 1
    )
    upright = jnp.concatenate([neighbours[:, :2], neighbours[:, 4:]], 1)
    down = jnp.any((upright == expected) & (upright >= 0))
    flags = jnp.concatenate(
        [
            jnp.concatenate([(neighbours >= 0).astype(jnp.int32), is_ocean[:, None]], 1),
            jnp.broadcast_to(down.astype(jnp.int32), (1, 9)),
        ],
        0,
    )
    taps = tap_matrices(kernel)
    flipped_taps = tap_matrices(kernel[::-1, ::-1])
    vectors = jnp.stack([conv_bias, ln_gain, ln_bias, layer_scale], 0)

    rv, rs, rc = exchange(pack(tiles, down), per_column, 0)

    smem = pl.BlockSpec(memory_space=pltpu.SMEM)
    one_tile = pl.BlockSpec((1, extent, extent, channels), lambda i: (i, 0, 0, 0))
    padded_width = 16 + extent
    scratch = [
        pltpu.VMEM((extent + 6, padded_width, channels), F32),
        pltpu.VMEM((7, (extent + 6) // 2, extent, 2 * channels), BF),
    ]
    out_shapes = (
        jax.ShapeDtypeStruct(tiles.shape, BF),
        jax.ShapeDtypeStruct((2, 28, 8, 2 * channels), F32),
        jax.ShapeDtypeStruct((channels, hidden), F32),
        jax.ShapeDtypeStruct((channels, hidden), F32),
        jax.ShapeDtypeStruct((4, 8, channels), F32),
        jax.ShapeDtypeStruct((8, hidden), F32),
    )
    operands = (taps, vectors, w_up, up_bias[None], w_down)
    grad_tiles, g_taps, g_up, g_down, g_vec, g_hidden = pl.pallas_call(
        first_kernel,
        grid=(slots,),
        out_shape=out_shapes,
        in_specs=[smem, whole(tiles.shape), one_tile]
        + [whole(part.shape) for part in (rv, rs, rc) + operands],
        out_specs=(one_tile,) + tuple(whole(shape.shape) for shape in out_shapes[1:]),
        scratch_shapes=scratch
        + [pltpu.VMEM((extent // (2 * PAIRS), 2 * channels, PAIRS * extent), BF)],
        compiler_params=pltpu.CompilerParams(vmem_limit_bytes=VMEM_BYTES),
    )(flags, tiles, cot, rv, rs, rc, *operands)

    tap_sums = jnp.sum(g_taps, 2).reshape(2, 7, 8, channels)
    tap_sums = tap_sums[0, :, :7] + tap_sums[1, :, 1:]
    strips = hidden // channels

    def stacked(matrix):
        return jnp.concatenate(
            [matrix[:, k * channels : (k + 1) * channels] for k in range(strips)], 0
        )

    def unstacked(rows):
        return jnp.concatenate(jnp.split(rows, strips, 0), 1)

    parts = [
        stacked(g_up),
        stacked(g_down),
        tap_sums.reshape(49, channels),
        jnp.sum(g_vec, 1),
        stacked(jnp.sum(g_hidden, 0)[None]),
    ]
    rv, rs, rc = exchange(pack(grad_tiles, down), per_column, 1)
    result = pl.pallas_call(
        second_kernel,
        grid=(slots,),
        out_shape=jax.ShapeDtypeStruct(tiles.shape, BF),
        in_specs=[smem, whole(tiles.shape), one_tile]
        + [whole(part.shape) for part in (rv, rs, rc, flipped_taps)],
        out_specs=one_tile,
        scratch_shapes=scratch,
        compiler_params=pltpu.CompilerParams(vmem_limit_bytes=VMEM_BYTES),
        cost_estimate=pl.CostEstimate(
            flops=2 * slots * extent * extent * 28 * channels * 2 * channels,
            bytes_accessed=8 * 1024 * 1024,
            transcendentals=0,
        ),
    )(flags, grad_tiles, cot, rv, rs, rc, flipped_taps)

    sums = sum_over_devices(jnp.concatenate(parts, 0), 2)
    pieces = []
    first = 0
    for part in parts:
        pieces.append(sums[first : first + part.shape[0]])
        first += part.shape[0]
    g_up, g_down = unstacked(pieces[0]), unstacked(pieces[1])
    tap_sums = pieces[2].reshape(7, 7, channels)
    g_vec = pieces[3]
    g_hidden = unstacked(pieces[4])[0]
    scale = 1.0 / math.sqrt(
        fields.shape[0] * lax.axis_size("dp") * slots * tile_count * extent * extent
    )
    g_down = g_down.T
    g_scale = jnp.sum(w_down.astype(F32) * g_down, 0) / layer_scale + down_bias * g_vec[3]
    return (
        result[None],
        jnp.transpose(tap_sums, (1, 0, 2)) * scale,
        g_vec[0] * scale,
        g_vec[1] * scale,
        g_vec[2] * scale,
        g_up * scale,
        g_hidden * scale,
        g_down * scale,
        g_vec[3] * layer_scale * scale,
        g_scale * scale,
    )


def solution(mesh):
    tiled = P("dp", "tile", None, None, None)
    placed = (tiled, tiled, P("tile"), P("tile", None)) + (P(),) * 9
    return jax.shard_map(
        local,
        mesh=mesh,
        in_specs=placed,
        out_specs=(tiled,) + (P(),) * 9,
        check_vma=False,
    )
```
